32 devices in a mesh: dp: 4 (over x, core), mp: 8 (over z, y).
Axes of the slice: x: 2, y: 2, z: 4, core: 2. Of those that a mesh axis runs over, the one named last changes fastest.
Arguments:
- tokens: bfloat16 [8192, 4608], P('mp', 'dp'), may hold values from -6 to 6
- kv_weight: bfloat16 [2, 4608, 1024], P(None, 'dp', 'mp'), may hold values from -0.125 to 0.125
- d_kv: bfloat16 [8192, 2, 1024], P('mp', None, 'dp'), may hold values from -6 to 6
Outputs:
- kv_out: bfloat16 [8192, 2, 1024], P('mp', None, 'dp')
- d_tokens: bfloat16 [8192, 4608], P('mp', 'dp')
- grad_kv: float32 [2, 4608, 1024], P(None, 'dp', 'mp')
The draws below stay inside these ranges and needn't reach their ends.
All inputs are finite; a program needn't handle non-finite values.
Results may differ from the reference program's by a relative error of at most 0.001.
Values may be sent and summed in bfloat16 or wider, within the bound.
A program may use at most 128 MiB of HBM per device.

```python
import jax
import jax.numpy as jnp

D = 4608
KVW = 1024
TOKENS = 8192


def raised(array, rng, source, target, shards_of, factor):
    owner, partner = [(jnp.arange(array.shape[position]) // (array.shape[position] // shards_of)).reshape([-1 if axis == position else 1 for axis in range(array.ndim)]) for position in (source, target)]
    chosen = jax.random.permutation(rng, shards_of)[partner]
    strong = (owner == chosen) | (owner == (partner + shards_of // 2) % shards_of)
    return jnp.where(strong, factor * array, array)


def steps_of(key, dims, split, smallest, largest):
    def one(position, parts):
        draws = jax.random.uniform(jax.random.fold_in(jax.random.fold_in(key, 6), position), (parts,), jnp.float32, smallest / len(split), largest / len(split))
        return jnp.repeat(jnp.exp(draws), dims[position] // parts).reshape((-1,) + (1,) * (len(dims) - position - 1))

    level = one(*split[0])
    for cut in split[1:]:
        level = level * one(*cut)
    return level


def noise(own_key, shape, scale, most, split=(), dtype=jnp.bfloat16):
    result = jax.random.normal(own_key, shape, jnp.float32) * scale
    if len(split) > 0:
        result = steps_of(own_key, shape, split, -0.22, 0.18) * result
    return jnp.clip(result, min=-most, max=most).astype(dtype)


def noise_with(key, dims, deviation, limit, pieces, heavy, held_as=jnp.bfloat16):
    values = deviation * jax.random.normal(key, dims, jnp.float32)
    if pieces:
        values = values * steps_of(key, dims, pieces, -0.22, 0.18)
    return jnp.clip(raised(values, jax.random.fold_in(key, 3), *heavy), -limit, limit).astype(held_as)


def setup_inputs(seed: int = 0) -> dict:
    seeds = jax.random.split(jax.random.key(seed), 4)
    tokens = noise(seeds[0], (TOKENS, D), 1.0, 6.0, ((0, 8), (1, 4)))
    kv_weight = noise_with(seeds[1], (2, D, KVW), D ** -0.5, 0.125, ((1, 4), (2, 8)), (1, 2, 8, 2.0))
    d_kv = noise_with(seeds[2], (TOKENS, 2, KVW), 1.0, 6.0, ((0, 8), (2, 4)), (0, 2, 8, 2.0))
    return dict(tokens=tokens, kv_weight=kv_weight, d_kv=d_kv)


def reference(tokens, kv_weight, d_kv):
    joined = jnp.transpose(kv_weight, (1, 0, 2)).reshape(D, 2 * KVW)
    kv_flat = jnp.dot(tokens, joined, preferred_element_type=jnp.float32)
    kv_out = kv_flat.astype(jnp.bfloat16).reshape(TOKENS, 2, KVW)
    d_flat = d_kv.reshape(TOKENS, 2 * KVW)
    d_tokens = jnp.dot(d_flat, joined.T, preferred_element_type=jnp.float32).astype(jnp.bfloat16)
    grad_flat = jnp.dot(tokens.T, d_flat, preferred_element_type=jnp.float32)
    grad_kv = jnp.transpose(grad_flat.reshape(D, 2, KVW), (1, 0, 2))
    return kv_out, d_tokens, grad_kv
```

```python
import jax
import jax.numpy as jnp
from jax import lax
from jax.sharding import PartitionSpec as P

F32, BF16, F16 = jnp.float32, jnp.bfloat16, jnp.float16


def general(tokens, kv_weight, d_kv):
    panels = lax.all_gather(kv_weight, "mp", axis=2, tiled=True)
    partial_value = jnp.einsum("td,kdc->tkc", tokens, panels, preferred_element_type=F32)
    kv_out = lax.psum_scatter(partial_value, "dp", scatter_dimension=2, tiled=True).astype(BF16)
    cotangent = lax.all_gather(d_kv, "dp", axis=2, tiled=True)
    d_tokens = jnp.einsum("tkc,kdc->td", cotangent, panels, preferred_element_type=F32).astype(BF16)
    partial_grad = jnp.einsum("td,tkc->ckd", tokens, cotangent, preferred_element_type=F32)
    owned_share = lax.psum_scatter(partial_grad, "mp", scatter_dimension=0, tiled=True)
    return kv_out, d_tokens, jnp.transpose(owned_share, (1, 2, 0))


def dot(a, b, ca, cb):
    return lax.dot_general(a, b, (((ca,), (cb,)), ((), ())), preferred_element_type=F32)


def hops(tokens, kv_weight, d_kv):
    rows, feats = tokens.shape
    wide = kv_weight.shape[2]
    me = lax.axis_index("dp")
    mp = lax.axis_index("mp")
    z, y = mp // 2, mp % 2
    pair = 4 * wide

    def over_z(a):
        return lax.ppermute(a, "mp", [(m, (m + 2) % 8) for m in range(8)])

    def over_y(a):
        return lax.ppermute(a, "mp", [(m, m ^ 1) for m in range(8)])

    def over_x(a):
        return lax.ppermute(a, "dp", [(d, d ^ 2) for d in range(4)])

    def over_core(a):
        return lax.ppermute(a, "dp", [(d, d ^ 1) for d in range(4)])

    def place(a, index):
        return lax.dynamic_slice(a, (0, index * pair), (a.shape[0], pair))

    most = jnp.stack([jnp.max(jnp.abs(tokens)), jnp.max(jnp.abs(d_kv))]).astype(F32)
    most = lax.pmax(most, ("dp", "mp"))
    bound = jnp.maximum(most[0] * most[1] * (rows * 8), 1e-30)
    down, up = 60000.0 / bound, bound / 60000.0

    block = jnp.transpose(kv_weight, (1, 0, 2)).reshape(feats, 2 * wide)
    ring = []
    for s in range(4):
        ring += [block, over_y(block)]
        if s < 3:
            block = over_z(block)

    halves = d_kv.reshape(rows, 2, 2, wide)
    halves = jnp.where(y == 0, halves, halves[:, :, ::-1])
    own = jnp.transpose(halves, (0, 2, 1, 3)).reshape(rows, pair)
    across = over_x(own)
    cot = jnp.concatenate([own, over_core(own), across, over_core(across)], axis=1)

    travelling = None
    for s in range(4):
        part = place(cot, me ^ ((z - 1 - s) % 4))
        away = dot(tokens, part[:, 2 * wide :], 0, 0)
        arrived = over_y((away * down).astype(F16))
        mine = dot(tokens, part[:, : 2 * wide], 0, 0) * down + arrived.astype(F32)
        if travelling is not None:
            mine = mine + travelling.astype(F32)
        if s < 3:
            travelling = over_z(mine.astype(F16))
    grad_kv = jnp.transpose((mine * up).reshape(feats, 2, wide), (1, 0, 2))

    panels = jnp.concatenate(ring, axis=1)
    panel = [place(panels, (z - (me ^ r)) % 4) for r in range(4)]
    far = over_core(dot(tokens, panel[3], 1, 0))
    far = over_x(dot(tokens, panel[2], 1, 0) + far)
    near = over_core(dot(tokens, panel[1], 1, 0))
    kv = dot(tokens, panel[0], 1, 0) + near + far
    kv = jnp.transpose(kv.reshape(rows, 2, 2, wide), (0, 2, 1, 3))
    kv = jnp.where(y == 0, kv, kv[:, :, ::-1])
    kv_out = kv.reshape(rows, 2, 2 * wide).astype(BF16)

    d_tokens = dot(cot, jnp.concatenate(panel, axis=1), 1, 1).astype(BF16)
    return kv_out, d_tokens, grad_kv


def solution(mesh):
    placed = (P("mp", "dp"), P(None, "dp", "mp"), P("mp", None, "dp"))

    def per_device(tokens, kv_weight, d_kv):
        fits = dict(mesh.shape) == {"dp": 4, "mp": 8} and kv_weight.shape[2] % 128 == 0
        return (hops if fits else general)(tokens, kv_weight, d_kv)

    return jax.shard_map(
        per_device,
        mesh=mesh,
        in_specs=placed,
        out_specs=(P("mp", None, "dp"), P("mp", "dp"), P(None, "dp", "mp")),
        check_vma=False,
    )
```

```python
import jax
import jax.numpy as jnp
from jax import lax
from jax.sharding import PartitionSpec as P

F32, BF16, F16 = jnp.float32, jnp.bfloat16, jnp.float16


def general(tokens, kv_weight, d_kv):
    panels = lax.all_gather(kv_weight, "mp", axis=2, tiled=True)
    partial_value = jnp.einsum("td,kdc->tkc", tokens, panels, preferred_element_type=F32)
    kv_out = lax.psum_scatter(partial_value, "dp", scatter_dimension=2, tiled=True).astype(BF16)
    cotangent = lax.all_gather(d_kv, "dp", axis=2, tiled=True)
    d_tokens = jnp.einsum("tkc,kdc->td", cotangent, panels, preferred_element_type=F32).astype(BF16)
    partial_grad = jnp.einsum("td,tkc->ckd", tokens, cotangent, preferred_element_type=F32)
    owned_share = lax.psum_scatter(partial_grad, "mp", scatter_dimension=0, tiled=True)
    return kv_out, d_tokens, jnp.transpose(owned_share, (1, 2, 0))


def dot(a, b, ca, cb):
    return lax.dot_general(a, b, (((ca,), (cb,)), ((), ())), preferred_element_type=F32)


def hops(tokens, kv_weight, d_kv):
    rows, feats = tokens.shape
    wide = kv_weight.shape[2]
    me = lax.axis_index("dp")
    mp = lax.axis_index("mp")
    z, y = mp // 2, mp % 2
    pair = 4 * wide

    def over_z(a):
        return lax.ppermute(a, "mp", [(m, (m + 2) % 8) for m in range(8)])

    def over_y(a):
        return lax.ppermute(a, "mp", [(m, m ^ 1) for m in range(8)])

    def over_x(a):
        return lax.ppermute(a, "dp", [(d, d ^ 2) for d in range(4)])

    def over_core(a):
        return lax.ppermute(a, "dp", [(d, d ^ 1) for d in range(4)])

    def place(a, index):
        return lax.dynamic_slice(a, (0, index * pair), (a.shape[0], pair))

    most = jnp.stack([jnp.max(jnp.abs(a)).astype(F32) for a in (tokens, d_kv, kv_weight)])
    for flip in (1, 2, 4):
        most = jnp.maximum(most, lax.ppermute(most, "mp", [(m, m ^ flip) for m in range(8)]))
    for flip in (1, 2):
        most = jnp.maximum(most, lax.ppermute(most, "dp", [(d, d ^ flip) for d in range(4)]))
    bound = jnp.maximum(most[0] * most[1] * (rows * 8), 1e-30)
    down, up = 60000.0 / bound, bound / 60000.0
    kv_bound = jnp.maximum(most[0] * most[2] * (feats * 2), 1e-30)
    kv_down, kv_up = 60000.0 / kv_bound, kv_bound / 60000.0

    block = jnp.transpose(kv_weight, (1, 0, 2)).reshape(feats, 2 * wide)
    ring = []
    for s in range(4):
        ring += [block, over_y(block)]
        if s < 3:
            block = over_z(block)

    both = jnp.transpose(d_kv, (1, 0, 2))
    low, high = both[:, :, :wide], both[:, :, wide:]
    first, second = jnp.where(y == 0, low, high), jnp.where(y == 0, high, low)
    own = jnp.concatenate([first[0], first[1], second[0], second[1]], axis=1)
    across = over_x(own)
    cot = jnp.concatenate([own, over_core(own), across, over_core(across)], axis=1)

    travelling = None
    for s in range(4):
        part = place(cot, me ^ ((z - 1 - s) % 4))
        away = dot(tokens, part[:, 2 * wide :], 0, 0)
        arrived = over_y((away * down).astype(F16))
        mine = dot(tokens, part[:, : 2 * wide], 0, 0) * down + arrived.astype(F32)
        if travelling is not None:
            mine = mine + travelling.astype(F32)
        if s < 3:
            travelling = over_z(mine.astype(F16))
    grad_kv = jnp.transpose((mine * up).reshape(feats, 2, wide), (1, 0, 2))

    panels = jnp.concatenate(ring, axis=1)
    panel = [place(panels, (z - (me ^ r)) % 4) for r in range(4)]
    far = over_core(dot(tokens, panel[3], 1, 0))
    far = over_x(((dot(tokens, panel[2], 1, 0) + far) * kv_down).astype(F16)).astype(F32) * kv_up
    near = over_core(dot(tokens, panel[1], 1, 0))
    kv = dot(tokens, panel[0], 1, 0) + near + far
    kv = jnp.transpose(kv.reshape(rows, 2, 2, wide), (0, 2, 1, 3))
    kv = jnp.where(y == 0, kv, kv[:, :, ::-1])
    kv_out = kv.reshape(rows, 2, 2 * wide).astype(BF16)

    d_tokens = dot(cot, jnp.concatenate(panel, axis=1), 1, 1).astype(BF16)
    return kv_out, d_tokens, grad_kv


def solution(mesh):
    placed = (P("mp", "dp"), P(None, "dp", "mp"), P("mp", None, "dp"))

    def per_device(tokens, kv_weight, d_kv):
        fits = dict(mesh.shape) == {"dp": 4, "mp": 8} and kv_weight.shape[2] % 128 == 0
        return (hops if fits else general)(tokens, kv_weight, d_kv)

    return jax.shard_map(
        per_device,
        mesh=mesh,
        in_specs=placed,
        out_specs=(P("mp", None, "dp"), P("mp", "dp"), P(None, "dp", "mp")),
        check_vma=False,
    )
```

```python
import jax
import jax.numpy as jnp
from jax import lax
from jax.sharding import PartitionSpec as P

F32, BF16, F16 = jnp.float32, jnp.bfloat16, jnp.float16


def general(tokens, kv_weight, d_kv):
    panels = lax.all_gather(kv_weight, "mp", axis=2, tiled=True)
    partial_value = jnp.einsum("td,kdc->tkc", tokens, panels, preferred_element_type=F32)
    kv_out = lax.psum_scatter(partial_value, "dp", scatter_dimension=2, tiled=True).astype(BF16)
    cotangent = lax.all_gather(d_kv, "dp", axis=2, tiled=True)
    d_tokens = jnp.einsum("tkc,kdc->td", cotangent, panels, preferred_element_type=F32).astype(BF16)
    partial_grad = jnp.einsum("td,tkc->ckd", tokens, cotangent, preferred_element_type=F32)
    owned_share = lax.psum_scatter(partial_grad, "mp", scatter_dimension=0, tiled=True)
    return kv_out, d_tokens, jnp.transpose(owned_share, (1, 2, 0))


def dot(a, b, ca, cb):
    return lax.dot_general(a, b, (((ca,), (cb,)), ((), ())), preferred_element_type=F32)


def after(value, *arrays):
    for a in arrays:
        value = value + 0.0 * a[0, 0].astype(F32)
    return value


def hops(tokens, kv_weight, d_kv):
    rows, feats = tokens.shape
    wide = kv_weight.shape[2]
    me = lax.axis_index("dp")
    mp = lax.axis_index("mp")
    z, y = mp // 2, mp % 2
    pair = 4 * wide

    def over_z(a):
        return lax.ppermute(a, "mp", [(m, (m + 2) % 8) for m in range(8)])

    def over_y(a):
        return lax.ppermute(a, "mp", [(m, m ^ 1) for m in range(8)])

    def over_x(a):
        return lax.ppermute(a, "dp", [(d, d ^ 2) for d in range(4)])

    def over_core(a):
        return lax.ppermute(a, "dp", [(d, d ^ 1) for d in range(4)])

    def place(a, index):
        return lax.dynamic_slice(a, (0, index * pair), (a.shape[0], pair))

    block = jnp.transpose(kv_weight, (1, 0, 2)).reshape(feats, 2 * wide)
    ring = []
    for s in range(4):
        ring += [block]
        if s < 3:
            ring += [over_y(block)]
            block = over_z(block)

    both = jnp.transpose(d_kv, (1, 0, 2))
    low, high = both[:, :, :wide], both[:, :, wide:]
    first, second = jnp.where(y == 0, low, high), jnp.where(y == 0, high, low)
    own = jnp.concatenate([first[0], first[1], second[0], second[1]], axis=1)
    across = over_x(own)
    cot = jnp.concatenate([own, over_core(own), across, over_core(across)], axis=1)

    most = jnp.stack([jnp.max(jnp.abs(a)).astype(F32) for a in (tokens, own, ring[0])])
    for flip in (1, 2):
        most = jnp.maximum(most, lax.ppermute(most, "dp", [(d, d ^ flip) for d in range(4)]))
    for flip in (1, 2, 4):
        if flip == 2:
            most = after(most, ring[2], across)
        most = jnp.maximum(most, lax.ppermute(most, "mp", [(m, m ^ flip) for m in range(8)]))
    bound = jnp.maximum(most[0] * most[1] * (rows * 8), 1e-30)
    down, up = 60000.0 / bound, bound / 60000.0
    kv_bound = jnp.maximum(most[0] * most[2] * (feats * 2), 1e-30)
    kv_down, kv_up = 60000.0 / kv_bound, kv_bound / 60000.0

    parts = [place(cot, me ^ ((z - 1 - s) % 4)) for s in range(4)]
    away = [(dot(tokens, p[:, 2 * wide :], 0, 0) * down).astype(F16) for p in parts]
    arrived = [over_y(a) for a in away]
    ring += [over_y(after(block.astype(F32), away[0], away[1]).astype(BF16))]

    panels = jnp.concatenate(ring, axis=1)
    panel = [place(panels, (z - (me ^ r)) % 4) for r in range(4)]
    far = over_core(dot(tokens, panel[3], 1, 0))
    far = ((dot(tokens, panel[2], 1, 0) + far) * kv_down).astype(F16)

    travelling = None
    for s, part in enumerate(parts):
        if s == 1:
            down = after(down, far)
        mine = dot(tokens, part[:, : 2 * wide], 0, 0) * down + arrived[s].astype(F32)
        if travelling is not None:
            mine = mine + travelling.astype(F32)
        if s < 3:
            travelling = over_z(mine.astype(F16))
    grad_kv = jnp.transpose((mine * up).reshape(feats, 2, wide), (1, 0, 2))

    far = over_x(far).astype(F32) * kv_up
    near = over_core(dot(tokens, panel[1], 1, 0))
    kv = dot(tokens, panel[0], 1, 0) + near + far
    kv = jnp.transpose(kv.reshape(rows, 2, 2, wide), (0, 2, 1, 3))
    kv = jnp.where(y == 0, kv, kv[:, :, ::-1])
    kv_out = kv.reshape(rows, 2, 2 * wide).astype(BF16)

    d_tokens = dot(cot, jnp.concatenate(panel, axis=1), 1, 1).astype(BF16)
    return kv_out, d_tokens, grad_kv


def solution(mesh):
    placed = (P("mp", "dp"), P(None, "dp", "mp"), P("mp", None, "dp"))

    def per_device(tokens, kv_weight, d_kv):
        fits = dict(mesh.shape) == {"dp": 4, "mp": 8} and kv_weight.shape[2] % 128 == 0
        return (hops if fits else general)(tokens, kv_weight, d_kv)

    return jax.shard_map(
        per_device,
        mesh=mesh,
        in_specs=placed,
        out_specs=(P("mp", None, "dp"), P("mp", "dp"), P(None, "dp", "mp")),
        check_vma=False,
    )
```

```python
import jax
import jax.numpy as jnp
from jax import lax
from jax.sharding import PartitionSpec as P

F32, BF16, F16 = jnp.float32, jnp.bfloat16, jnp.float16
SPAN = 60000.0


def general(tokens, kv_weight, d_kv):
    panels = lax.all_gather(kv_weight, "mp", axis=2, tiled=True)
    partial_value = jnp.einsum("td,kdc->tkc", tokens, panels, preferred_element_type=F32)
    kv_out = lax.psum_scatter(partial_value, "dp", scatter_dimension=2, tiled=True).astype(BF16)
    cotangent = lax.all_gather(d_kv, "dp", axis=2, tiled=True)
    d_tokens = jnp.einsum("tkc,kdc->td", cotangent, panels, preferred_element_type=F32).astype(BF16)
    partial_grad = jnp.einsum("td,tkc->ckd", tokens, cotangent, preferred_element_type=F32)
    owned_share = lax.psum_scatter(partial_grad, "mp", scatter_dimension=0, tiled=True)
    return kv_out, d_tokens, jnp.transpose(owned_share, (1, 2, 0))


def dot(a, b, ca, cb):
    return lax.dot_general(a, b, (((ca,), (cb,)), ((), ())), preferred_element_type=F32)


def after(value, *arrays):
    for a in arrays:
        value = value + 0.0 * a[0, 0].astype(F32)
    return value


def hops(tokens, kv_weight, d_kv):
    rows, feats = tokens.shape
    wide = kv_weight.shape[2]
    me = lax.axis_index("dp")
    mp = lax.axis_index("mp")
    z, y = mp // 2, mp % 2
    pair = 4 * wide

    def over_z(a):
        return lax.ppermute(a, "mp", [(m, (m + 2) % 8) for m in range(8)])

    def over_y(a):
        return lax.ppermute(a, "mp", [(m, m ^ 1) for m in range(8)])

    def over_x(a):
        return lax.ppermute(a, "dp", [(d, d ^ 2) for d in range(4)])

    def over_core(a):
        return lax.ppermute(a, "dp", [(d, d ^ 1) for d in range(4)])

    def place(a, index):
        return lax.dynamic_slice(a, (0, index * pair), (a.shape[0], pair))

    block = jnp.transpose(kv_weight, (1, 0, 2)).reshape(feats, 2 * wide)
    ring = []
    for s in range(4):
        ring += [block]
        if s < 3:
            ring += [over_y(block)]
            block = over_z(block)

    both = jnp.transpose(d_kv, (1, 0, 2))
    low, high = both[:, :, :wide], both[:, :, wide:]
    first, second = jnp.where(y == 0, low, high), jnp.where(y == 0, high, low)
    own = jnp.concatenate([first[0], first[1], second[0], second[1]], axis=1)
    across = over_x(own)
    cot = jnp.concatenate([own, over_core(own), across, over_core(across)], axis=1)

    most = [jnp.max(jnp.abs(a)).astype(F32) for a in (tokens, cot)]
    bound = jnp.maximum(most[0] * most[1] * rows, 1e-30)[None]
    beside = over_y(bound)
    shifts = (2, 1, 3, 0)
    parts = [place(cot, me ^ ((z + r) % 4)) for r in shifts]
    away = [(dot(tokens, p[:, 2 * wide :], 0, 0) * (SPAN / bound)).astype(F16) for p in parts]
    arrived = [over_y(a) for a in away]
    total = bound + beside
    for flip in (2, 4):
        total = total + lax.ppermute(total, "mp", [(m, m ^ flip) for m in range(8)])
    ring += [over_y(after(block.astype(F32), away[0], away[1], total[None]).astype(BF16))]

    panels = jnp.concatenate(ring, axis=1)
    panel = [place(panels, (z - (me ^ r)) % 4) for r in range(4)]
    far = over_core(after(dot(tokens, panel[3], 1, 0), arrived[0], arrived[1]))
    far = dot(tokens, panel[2], 1, 0) + far
    far_most = jnp.maximum(jnp.max(jnp.abs(far)), 1e-30)[None]
    far = (far * (SPAN / far_most)).astype(F16)

    far_beside = over_x(far_most)
    landed = []
    for r, part, other in zip(shifts, parts, arrived):
        if r == 0:
            beside = after(beside, far_beside[None])
        mine = dot(tokens, part[:, : 2 * wide], 0, 0) + other.astype(F32) * (beside / SPAN)
        if r:
            sent = (mine * (SPAN / total)).astype(F16)
            landed += [lax.ppermute(sent, "mp", [(m, (m + 2 * r) % 8) for m in range(8)])]
    for share in landed:
        mine = mine + share.astype(F32) * (total / SPAN)
    grad_kv = jnp.transpose(mine.reshape(feats, 2, wide), (1, 0, 2))

    far = over_x(far).astype(F32) * (far_beside / SPAN)
    near = over_core(dot(tokens, panel[1], 1, 0))
    kv = dot(tokens, panel[0], 1, 0) + near + far
    kv = jnp.transpose(kv.reshape(rows, 2, 2, wide), (0, 2, 1, 3))
    kv = jnp.where(y == 0, kv, kv[:, :, ::-1])
    kv_out = kv.reshape(rows, 2, 2 * wide).astype(BF16)

    d_tokens = dot(cot, jnp.concatenate(panel, axis=1), 1, 1).astype(BF16)
    return kv_out, d_tokens, grad_kv


def solution(mesh):
    placed = (P("mp", "dp"), P(None, "dp", "mp"), P("mp", None, "dp"))

    def per_device(tokens, kv_weight, d_kv):
        fits = dict(mesh.shape) == {"dp": 4, "mp": 8} and kv_weight.shape[2] % 128 == 0
        return (hops if fits else general)(tokens, kv_weight, d_kv)

    return jax.shard_map(
        per_device,
        mesh=mesh,
        in_specs=placed,
        out_specs=(P("mp", None, "dp"), P("mp", "dp"), P(None, "dp", "mp")),
        check_vma=False,
    )
```

```python
import jax
import jax.numpy as jnp
from jax import lax
from jax.sharding import PartitionSpec as P

F32, BF16, F16 = jnp.float32, jnp.bfloat16, jnp.float16
SPAN = 60000.0


def general(tokens, kv_weight, d_kv):
    panels = lax.all_gather(kv_weight, "mp", axis=2, tiled=True)
    partial_value = jnp.einsum("td,kdc->tkc", tokens, panels, preferred_element_type=F32)
    kv_out = lax.psum_scatter(partial_value, "dp", scatter_dimension=2, tiled=True).astype(BF16)
    cotangent = lax.all_gather(d_kv, "dp", axis=2, tiled=True)
    d_tokens = jnp.einsum("tkc,kdc->td", cotangent, panels, preferred_element_type=F32).astype(BF16)
    partial_grad = jnp.einsum("td,tkc->ckd", tokens, cotangent, preferred_element_type=F32)
    owned_share = lax.psum_scatter(partial_grad, "mp", scatter_dimension=0, tiled=True)
    return kv_out, d_tokens, jnp.transpose(owned_share, (1, 2, 0))


def dot(a, b, ca, cb):
    return lax.dot_general(a, b, (((ca,), (cb,)), ((), ())), preferred_element_type=F32)


def after(value, *arrays):
    for a in arrays:
        value = value + 0.0 * a[0, 0].astype(F32)
    return value


def hops(tokens, kv_weight, d_kv):
    rows, feats = tokens.shape
    wide = kv_weight.shape[2]
    me = lax.axis_index("dp")
    mp = lax.axis_index("mp")
    z, y = mp // 2, mp % 2
    pair = 4 * wide

    def over_z(a):
        return lax.ppermute(a, "mp", [(m, (m + 2) % 8) for m in range(8)])

    def over_y(a):
        return lax.ppermute(a, "mp", [(m, m ^ 1) for m in range(8)])

    def over_x(a):
        return lax.ppermute(a, "dp", [(d, d ^ 2) for d in range(4)])

    def over_core(a):
        return lax.ppermute(a, "dp", [(d, d ^ 1) for d in range(4)])

    def place(a, index):
        return lax.dynamic_slice(a, (0, index * pair), (a.shape[0], pair))

    block = jnp.transpose(kv_weight, (1, 0, 2)).reshape(feats, 2 * wide)
    ring = []
    for s in range(4):
        ring += [block]
        if s < 3:
            ring += [over_y(block)]
            block = over_z(block)

    both = jnp.transpose(d_kv, (1, 0, 2))
    low, high = both[:, :, :wide], both[:, :, wide:]
    first, second = jnp.where(y == 0, low, high), jnp.where(y == 0, high, low)
    own = jnp.concatenate([first[0], first[1], second[0], second[1]], axis=1)
    across = over_x(own)
    cot = jnp.concatenate([own, over_core(own), across, over_core(across)], axis=1)

    most = [jnp.max(jnp.abs(a)).astype(F32) for a in (tokens, cot)]
    bound = jnp.maximum(most[0] * most[1] * rows, 1e-30)[None]
    beside = over_y(bound)
    shifts = (2, 1, 3, 0)
    parts = [place(cot, me ^ ((z + r) % 4)) for r in shifts]
    away = [(dot(tokens, p[:, 2 * wide :], 0, 0) * (SPAN / bound)).astype(F16) for p in parts]
    arrived = [over_y(a) for a in away]
    total = bound + beside
    for flip in (2, 4):
        total = total + lax.ppermute(total, "mp", [(m, m ^ flip) for m in range(8)])
    ring += [over_y(block)]

    panels = jnp.concatenate(ring, axis=1)
    panel = [place(panels, (z - (me ^ r)) % 4) for r in range(4)]
    far = over_core(dot(tokens, panel[3], 1, 0))
    far = dot(tokens, panel[2], 1, 0) + far
    share_most = jnp.max(jnp.abs(panels)).astype(F32) * most[0] * feats
    share_most = jnp.maximum(share_most, 1e-30)[None]
    far_most = share_most + over_core(share_most)
    far = (far * (SPAN / far_most)).astype(F16)

    far_beside = over_x(far_most)
    landed = []
    for r, part, other in zip(shifts, parts, arrived):
        if r == 1:
            beside = after(beside, far, far_beside[None])
        mine = dot(tokens, part[:, : 2 * wide], 0, 0) + other.astype(F32) * (beside / SPAN)
        if r:
            sent = (mine * (SPAN / total)).astype(F16)
            landed += [lax.ppermute(sent, "mp", [(m, (m + 2 * r) % 8) for m in range(8)])]
    for share in landed:
        mine = mine + share.astype(F32) * (total / SPAN)
    grad_kv = jnp.transpose(mine.reshape(feats, 2, wide), (1, 0, 2))

    far = over_x(far).astype(F32) * (far_beside / SPAN)
    near = over_core(dot(tokens, panel[1], 1, 0))
    kv = dot(tokens, panel[0], 1, 0) + near + far
    kv = jnp.transpose(kv.reshape(rows, 2, 2, wide), (0, 2, 1, 3))
    kv = jnp.where(y == 0, kv, kv[:, :, ::-1])
    kv_out = kv.reshape(rows, 2, 2 * wide).astype(BF16)

    d_tokens = dot(cot, jnp.concatenate(panel, axis=1), 1, 1).astype(BF16)
    return kv_out, d_tokens, grad_kv


def solution(mesh):
    placed = (P("mp", "dp"), P(None, "dp", "mp"), P("mp", None, "dp"))

    def per_device(tokens, kv_weight, d_kv):
        fits = dict(mesh.shape) == {"dp": 4, "mp": 8} and kv_weight.shape[2] % 128 == 0
        return (hops if fits else general)(tokens, kv_weight, d_kv)

    return jax.shard_map(
        per_device,
        mesh=mesh,
        in_specs=placed,
        out_specs=(P("mp", None, "dp"), P("mp", "dp"), P(None, "dp", "mp")),
        check_vma=False,
    )
```
